128 devices in a mesh: deme: 16 (over y, z), gen: 8 (over x, core).
Axes of the slice: x: 4, y: 4, z: 4, core: 2. Of those that a mesh axis runs over, the one named last changes fastest.
Arguments:
- freqs: float32 [4096, 256, 512], P('deme', 'gen'), may hold values from 0 to 1
- start_basis: float32 [512, 128], replicated, may hold values from -0.25 to 0.25
Outputs:
- core: float32 [4096, 256, 128], P('deme', 'gen')
- factor: float32 [512, 128], replicated
The draws below stay inside these ranges and needn't reach their ends.
All inputs are finite; a program needn't handle non-finite values.
Results may differ from the reference program's by a relative error of at most 0.0003.
Values sent between devices are 32-bit elements; how exact they have to be, the bound alone decides.
No kernel may reach another device: no remote copies, remote signals or barrier semaphores. Data moves between devices by JAX's collectives and lax.ppermute only.
A program may use at most 64 MiB of HBM per device.

```python
import jax
import jax.numpy as jnp
from jax import lax

LOCI = 512
RANK = 128
ITERS = 4
DEMES = 4096
GENS = 256


def draw_freqs(key, part):
    key = jax.random.fold_in(key, 7)
    subkeys = jax.random.split(key, 9)
    factors = 16
    errors = jax.random.normal(subkeys[0], (DEMES, GENS, LOCI + 1), jnp.float32)
    roughness = jax.random.normal(subkeys[1], (factors, DEMES, GENS), jnp.float32)
    linkage = jax.random.uniform(subkeys[2], (LOCI,), jnp.float32, -0.7, 0.7)
    loading = jax.random.normal(subkeys[3], (factors, LOCI), jnp.float32)
    offset = jax.random.uniform(subkeys[4], (LOCI,), jnp.float32, -1.5, 1.5)
    locus_scale = jnp.exp(jax.random.uniform(subkeys[5], (LOCI,), jnp.float32, jnp.log(0.25), 0.0))
    wavenumber = jax.random.uniform(subkeys[6], (factors,), jnp.float32, 0.5, 3.0)
    phases = jax.random.uniform(subkeys[7], (factors,), jnp.float32, -jnp.pi, jnp.pi)
    drifts = jax.random.uniform(subkeys[8], (factors,), jnp.float32, -2.0, 2.0)
    position = (jnp.arange(DEMES, dtype=jnp.float32) + 0.5) / DEMES
    elapsed = (jnp.arange(GENS, dtype=jnp.float32) + 0.5) / GENS
    amplitude = 0.42 * jnp.power(0.85, jnp.arange(factors, dtype=jnp.float32))
    angle_part = 2.0 * jnp.pi * wavenumber[:, None, None] * position[None, :, None] + phases[:, None, None] + drifts[:, None, None] * elapsed[None, None, :]
    ancestry = amplitude[:, None, None] * (jnp.sin(angle_part) + 0.8 * roughness)
    logits = offset[None, None, :] + errors[:, :, 1:] + linkage[None, None, :] * errors[:, :, :-1]
    for index in range(factors):
        logits = logits + ancestry[index][:, :, None] * loading[index][None, None, :]
    return locus_scale[None, None, :] * jax.nn.sigmoid(logits)


def normal_values(own_key, dims, spread, limit, kind=jnp.bfloat16):
    values = jax.random.normal(own_key, dims, jnp.float32) * spread
    return jnp.minimum(jnp.maximum(values, -limit), limit).astype(kind)


def setup_inputs(seed: int = 0) -> dict:
    arg_keys = jax.random.split(jax.random.key(seed), 3)
    freqs = draw_freqs(jax.random.fold_in(arg_keys[2], 71), 0)
    start_basis = normal_values(arg_keys[1], (LOCI, RANK), LOCI ** -0.5, 0.25, jnp.float32)
    return {"freqs": freqs, "start_basis": start_basis}


def orthonormal(z):
    small = jnp.dot(z.T.astype(jnp.float32), z.astype(jnp.float32), precision=lax.Precision.HIGHEST, preferred_element_type=jnp.float32)
    lower = jnp.linalg.cholesky(small)
    return jax.scipy.linalg.solve_triangular(lower, z.T, lower=True).T

def reference(freqs, start_basis):
    mean = jnp.sum(freqs, axis=0) / DEMES
    centered = freqs - mean
    rows = centered.reshape(DEMES * GENS, LOCI)
    gram = lax.dot_general(rows.astype(jnp.float32), rows.astype(jnp.float32), (((0,), (0,)), ((), ())), precision=lax.Precision.HIGHEST, preferred_element_type=jnp.float32)
    gram = gram * (1.0 / (DEMES * GENS))
    basis = start_basis
    for step in range(ITERS):
        basis = orthonormal(jnp.dot(gram.astype(jnp.float32), basis.astype(jnp.float32), precision=lax.Precision.HIGHEST, preferred_element_type=jnp.float32))
    core = jnp.dot(rows.astype(jnp.float32), basis.astype(jnp.float32), precision=lax.Precision.HIGHEST, preferred_element_type=jnp.float32)
    return (core.reshape(DEMES, GENS, RANK), basis)
```

```python
import jax
import jax.numpy as jnp
from jax import lax
from jax.experimental import pallas as pl
from jax.experimental.pallas import tpu as pltpu
from jax.sharding import PartitionSpec as P

ITERS = 4
LOCI = 512
RANK = 128
BLOCK = 128
PIECE = 80
PACKED = 1280
PAIRS = [(i, j) for i in range(4) for j in range(i, 4)]
DEMES = 256
GENS = 32
CHUNK = 32
MEAN_ROWS = 128
AXES = ("deme", "gen")
MIB = 1024 * 1024


def place():
    deme, gen = lax.axis_index("deme"), lax.axis_index("gen")
    y, z, core = deme // 4, deme % 4, gen % 2
    return jnp.where(core == 0, z, y), jnp.where(core == 0, y, z), core


def piece_row(core, first, second):
    return PIECE * jnp.where(core == 0, 4 * first + second, 4 * second + first)


def shifted(kind, k):
    pairs = []
    for device in range(128):
        deme, gen = divmod(device, 8)
        y, z = divmod(deme, 4)
        x, core = divmod(gen, 2)
        if kind == "x":
            x = (x + k) % 4
        elif kind == "core":
            core = 1 - core
        elif (kind == "first") == (core == 0):
            z = (z + k) % 4
        else:
            y = (y + k) % 4
        pairs.append((device, (4 * y + z) * 8 + 2 * x + core))
    return pairs


def send(value, kind, k):
    return lax.ppermute(value, AXES, shifted(kind, k))


def cross(a, b, precision=None):
    return lax.dot_general(
        a, b, (((0,), (0,)), ((), ())), precision=precision, preferred_element_type=jnp.float32
    )


def gram_kernel(x_ref, *refs):
    outs, (split, top, low, shift, total, packed) = refs[:4], refs[4:]
    step = pl.program_id(0)

    @pl.when(step == 0)
    def _():
        shift[...] = jnp.sum(x_ref[...], axis=0) * (1.0 / CHUNK)
        total[...] = jnp.zeros_like(total)
        top[...] = jnp.zeros_like(top)
        low[...] = jnp.zeros_like(low)

    d = x_ref[...] - shift[...][None]
    total[...] += jnp.sum(d, axis=0)
    d = d.reshape(CHUNK * GENS, LOCI)
    hi = d.astype(jnp.bfloat16)
    split[:, :LOCI] = hi
    split[:, LOCI:] = (d - hi.astype(jnp.float32)).astype(jnp.bfloat16)
    top[...] += cross(split[:, :256], split[...])
    low[...] += cross(split[:, 256:512], split[:, 256:])

    @pl.when(step == pl.num_programs(0) - 1)
    def _():
        sums = total[...]
        offset = cross(sums, sums, lax.Precision.HIGHEST) * (1.0 / DEMES)

        def high(i, j):
            if i < 2:
                return top[BLOCK * i : BLOCK * (i + 1), BLOCK * j : BLOCK * (j + 1)]
            return low[BLOCK * (i - 2) : BLOCK * (i - 1), BLOCK * (j - 2) : BLOCK * (j - 1)]

        def mixed(i, j):
            if i < 2:
                return top[BLOCK * i : BLOCK * (i + 1), LOCI + BLOCK * j : LOCI + BLOCK * (j + 1)]
            return low[BLOCK * (i - 2) : BLOCK * (i - 1), 256 + BLOCK * j : 256 + BLOCK * (j + 1)]

        for n, (i, j) in enumerate(PAIRS):
            block = high(i, j) + (mixed(i, j) + mixed(j, i).T)
            packed[BLOCK * n : BLOCK * (n + 1), :] = (
                block - offset[BLOCK * i : BLOCK * (i + 1), BLOCK * j : BLOCK * (j + 1)]
            )
        mean = shift[...] + sums * (1.0 / DEMES)
        first, second, core = place()
        for k, out in enumerate(outs):
            to = (first + k) % 4
            for j in range(4):
                row = pl.multiple_of(piece_row(core, to, j), 8)
                out[PIECE * j : PIECE * (j + 1), :] = packed[pl.ds(row, PIECE), :]
                out[4 * PIECE + 32 * j : 4 * PIECE + 32 * (j + 1), :] = mean[:, BLOCK * j : BLOCK * (j + 1)]


def local_gram(freqs):
    rows = 4 * PIECE + MEAN_ROWS
    return pl.pallas_call(
        gram_kernel,
        grid=(DEMES // CHUNK,),
        in_specs=[pl.BlockSpec((CHUNK, GENS, LOCI), lambda t: (t, 0, 0))],
        out_specs=[pl.BlockSpec((rows, BLOCK), lambda t: (0, 0))] * 4,
        out_shape=[jax.ShapeDtypeStruct((rows, BLOCK), jnp.float32)] * 4,
        scratch_shapes=[
            pltpu.VMEM((CHUNK * GENS, 2 * LOCI), jnp.bfloat16),
            pltpu.VMEM((256, 1024), jnp.float32),
            pltpu.VMEM((256, 768), jnp.float32),
            pltpu.VMEM((GENS, LOCI), jnp.float32),
            pltpu.VMEM((GENS, LOCI), jnp.float32),
            pltpu.VMEM((PACKED, BLOCK), jnp.float32),
        ],
        compiler_params=pltpu.CompilerParams(vmem_limit_bytes=40 * MIB),
        cost_estimate=pl.CostEstimate(flops=2 * 8192 * 512 * 900, bytes_accessed=20 * MIB, transcendentals=0),
        name="local_gram",
    )(freqs)


def merge(refs, rows, weight, packed):
    wide = [
        jnp.concatenate([ref[rows + 32 * j : rows + 32 * (j + 1), :] for j in range(4)], axis=1) for ref in refs
    ]
    mean = ((wide[0] + wide[2]) + (wide[1] + wide[3])) * 0.25
    delta = jnp.concatenate([part - mean for part in wide], axis=0)
    for i in range(4):
        product = cross(delta[:, BLOCK * i : BLOCK * (i + 1)], delta[:, BLOCK * i :], lax.Precision.HIGHEST)
        for j in range(i, 4):
            n = PAIRS.index((i, j))
            packed[BLOCK * n : BLOCK * (n + 1), :] = product[:, BLOCK * (j - i) : BLOCK * (j - i + 1)] * weight
    return mean


def first_kernel(*refs):
    ins, outs, (packed, summed) = refs[:4], refs[4:8], refs[8:]
    mean = merge(ins, 4 * PIECE, float(DEMES), packed)
    first, second, core = place()
    for j in range(4):
        rows = slice(PIECE * j, PIECE * (j + 1))
        row = pl.multiple_of(piece_row(core, first, j), 8)
        summed[rows, :] = ((ins[0][rows, :] + ins[2][rows, :]) + (ins[1][rows, :] + ins[3][rows, :])) + packed[
            pl.ds(row, PIECE), :
        ]
    for k, out in enumerate(outs):
        row = pl.multiple_of(PIECE * ((second + k) % 4), 8)
        out[:PIECE, :] = summed[pl.ds(row, PIECE), :]
        for j in range(4):
            out[PIECE + 32 * j : PIECE + 32 * (j + 1), :] = mean[:, BLOCK * j : BLOCK * (j + 1)]


def second_kernel(*refs):
    ins, (out, mean_out), (packed,) = refs[:4], refs[4:6], refs[6:]
    mean_out[...] = merge(ins, PIECE, 4.0 * DEMES, packed)
    first, second, core = place()
    row = pl.multiple_of(piece_row(core, first, second), 8)
    rows = slice(0, PIECE)
    out[...] = ((ins[0][rows, :] + ins[2][rows, :]) + (ins[1][rows, :] + ins[3][rows, :])) + packed[
        pl.ds(row, PIECE), :
    ]


def merge_first(parts):
    rows = PIECE + MEAN_ROWS
    return pl.pallas_call(
        first_kernel,
        out_shape=[jax.ShapeDtypeStruct((rows, BLOCK), jnp.float32)] * 4,
        scratch_shapes=[pltpu.VMEM((PACKED, BLOCK), jnp.float32), pltpu.VMEM((4 * PIECE, BLOCK), jnp.float32)],
        compiler_params=pltpu.CompilerParams(vmem_limit_bytes=16 * MIB),
        name="merge_first",
    )(*parts)


def merge_second(parts):
    return pl.pallas_call(
        second_kernel,
        out_shape=[
            jax.ShapeDtypeStruct((PIECE, BLOCK), jnp.float32),
            jax.ShapeDtypeStruct((GENS, LOCI), jnp.float32),
        ],
        scratch_shapes=[pltpu.VMEM((PACKED, BLOCK), jnp.float32)],
        compiler_params=pltpu.CompilerParams(vmem_limit_bytes=16 * MIB),
        name="merge_second",
    )(*parts)


def inverse_cholesky(s):
    full = (8, RANK)
    lane = lax.broadcasted_iota(jnp.int32, full, 1)
    sub = lax.broadcasted_iota(jnp.int32, full, 0)
    count = RANK // 8
    rows = [s[8 * i : 8 * i + 8, :] for i in range(count)]
    for k in range(count):
        cols = {
            i: [jnp.broadcast_to(rows[i][:, 8 * k + j : 8 * k + j + 1], full) for j in range(8)]
            for i in range(k, count)
        }
        inverses = []
        for j in range(8):
            pivot = cols[k][j]
            inverse = 1.0 / jnp.broadcast_to(pivot[j : j + 1, :], full)
            inverses.append(inverse)
            for l in range(j + 1, 8):
                ratio = jnp.broadcast_to(pivot[l : l + 1, :], full) * inverse
                for i in range(k, count):
                    cols[i][l] = cols[i][l] - cols[i][j] * ratio
        here = (lane >= 8 * k) & (lane < 8 * k + 8)
        own = jnp.where(here, jnp.where(lane - 8 * k == sub, 1.0, 0.0), rows[k])
        scaled = []
        scale = inverses[0]
        for j in range(8):
            scaled.append(jnp.broadcast_to(own[j : j + 1, :], full) * inverses[j])
            if j < 7:
                own = own - jnp.where(sub > j, cols[k][j], 0.0) * scaled[j]
            if j:
                scale = jnp.where(sub == j, inverses[j], scale)
        for i in range(k + 1, count):
            rest = jnp.where(here, 0.0, rows[i])
            for j in range(8):
                rest = rest - cols[i][j] * scaled[j]
            rows[i] = rest
        rows[k] = jnp.where(lane <= 8 * k + sub, own * jnp.sqrt(scale), 0.0)
    return jnp.concatenate(rows, axis=0)


STEP = 16
STEPS = DEMES // STEP
LOADS = 4


def core_kernel(p0, p1, p2, p3, start_ref, mean_ref, x_hbm, core_hbm, factor_ref, x, core, packed, gram, loads, stores):
    def load(n):
        part = pl.ds(n * (DEMES // LOADS), DEMES // LOADS)
        return pltpu.make_async_copy(x_hbm.at[part], x.at[part], loads.at[n])

    def store(n):
        part = pl.ds(n * STEP, STEP)
        return pltpu.make_async_copy(core.at[part], core_hbm.at[part], stores.at[n])

    for n in range(LOADS):
        load(n).start()

    first, second, core_id = place()
    for k, part in enumerate((p0, p1, p2, p3)):
        for l in range(4):
            row = pl.multiple_of(piece_row(core_id, (first + 4 - k) % 4, (second + 4 - l) % 4), 8)
            packed[pl.ds(row, PIECE), :] = part[PIECE * l : PIECE * (l + 1), :]
    for n, (i, j) in enumerate(PAIRS):
        block = packed[BLOCK * n : BLOCK * (n + 1), :] * (1.0 / (4096 * 256))
        gram[BLOCK * i : BLOCK * (i + 1), BLOCK * j : BLOCK * (j + 1)] = block
        if i != j:
            gram[BLOCK * j : BLOCK * (j + 1), BLOCK * i : BLOCK * (i + 1)] = block.T

    def body(_, basis):
        z = jnp.dot(basis, gram[...], precision=lax.Precision.HIGHEST, preferred_element_type=jnp.float32)
        small = lax.dot_general(
            z, z, (((1,), (1,)), ((), ())), precision=lax.Precision.HIGHEST, preferred_element_type=jnp.float32
        )
        return jnp.dot(
            inverse_cholesky(small), z, precision=lax.Precision.HIGHEST, preferred_element_type=jnp.float32
        )

    basis = lax.fori_loop(0, ITERS, body, start_ref[...].T)
    factor = basis.T
    factor_ref[...] = factor
    hi = factor.astype(jnp.bfloat16)
    lo = (factor - hi.astype(jnp.float32)).astype(jnp.bfloat16)
    both = jnp.concatenate([hi, lo], axis=1)
    mean = mean_ref[...]
    for n in range(LOADS):
        load(n).wait()

    def step(n, carry):
        part = pl.ds(n * STEP, STEP)
        d = (x[part] - mean[None]).reshape(STEP * GENS, LOCI)
        d_hi = d.astype(jnp.bfloat16)
        d_lo = (d - d_hi.astype(jnp.float32)).astype(jnp.bfloat16)
        wide = jnp.dot(d_hi, both, preferred_element_type=jnp.float32)
        rest = jnp.dot(d_lo, hi, preferred_element_type=jnp.float32)
        core[part] = (wide[:, :RANK] + (wide[:, RANK:] + rest)).reshape(STEP, GENS, RANK)
        store(n).start()
        return carry

    lax.fori_loop(0, STEPS, step, 0)
    for n in range(STEPS):
        store(n).wait()


def iterate(parts, start_basis, mean, freqs):
    vmem = pl.BlockSpec(memory_space=pltpu.VMEM)
    hbm = pl.BlockSpec(memory_space=pltpu.HBM)
    return pl.pallas_call(
        core_kernel,
        in_specs=[vmem] * 6 + [hbm],
        out_specs=[hbm, vmem],
        out_shape=[
            jax.ShapeDtypeStruct((DEMES, GENS, RANK), jnp.float32),
            jax.ShapeDtypeStruct((LOCI, RANK), jnp.float32),
        ],
        scratch_shapes=[
            pltpu.VMEM((DEMES, GENS, LOCI), jnp.float32),
            pltpu.VMEM((DEMES, GENS, RANK), jnp.float32),
            pltpu.VMEM((PACKED, BLOCK), jnp.float32),
            pltpu.VMEM((LOCI, LOCI), jnp.float32),
            pltpu.SemaphoreType.DMA((LOADS,)),
            pltpu.SemaphoreType.DMA((STEPS,)),
        ],
        compiler_params=pltpu.CompilerParams(vmem_limit_bytes=48 * MIB),
        name="iterate",
    )(*parts, start_basis, mean, freqs)


def local(freqs, start_basis):
    out = local_gram(freqs)
    parts = merge_first([out[0]] + [send(out[k], "first", k) for k in (1, 2, 3)])
    shard, mean = merge_second([parts[0]] + [send(parts[k], "second", k) for k in (1, 2, 3)])
    one, two, three = [send(shard, "x", k) for k in (1, 2, 3)]
    shard = (shard + two) + (one + three)
    shard = shard + send(shard, "core", 1)
    row = jnp.concatenate([shard] + [send(shard, "second", k) for k in (1, 2, 3)], axis=0)
    rows = [row] + [send(row, "first", k) for k in (1, 2, 3)]
    return tuple(iterate(rows, start_basis, mean, freqs))


def solution(mesh):
    in_specs = (P("deme", "gen", None), P())
    out_specs = (P("deme", "gen", None), P())
    return jax.shard_map(local, mesh=mesh, in_specs=in_specs, out_specs=out_specs, check_vma=False)
```

```python
import jax
import jax.numpy as jnp
from jax import lax
from jax.experimental import pallas as pl
from jax.experimental.pallas import tpu as pltpu
from jax.sharding import PartitionSpec as P

ITERS = 4
LOCI = 512
RANK = 128
BLOCK = 128
PIECE = 80
PACKED = 1280
PAIRS = [(i, j) for i in range(4) for j in range(i, 4)]
DEMES = 256
GENS = 32
CHUNK = 32
MEAN_ROWS = 128
AXES = ("deme", "gen")
MIB = 1024 * 1024


def place():
    deme, gen = lax.axis_index("deme"), lax.axis_index("gen")
    y, z, core = deme // 4, deme % 4, gen % 2
    return jnp.where(core == 0, z, y), jnp.where(core == 0, y, z), core


def piece_row(core, first, second):
    return PIECE * jnp.where(core == 0, 4 * first + second, 4 * second + first)


def shifted(kind, k):
    pairs = []
    for device in range(128):
        deme, gen = divmod(device, 8)
        y, z = divmod(deme, 4)
        x, core = divmod(gen, 2)
        if kind == "x":
            x = (x + k) % 4
        elif kind == "core":
            core = 1 - core
        elif (kind == "first") == (core == 0):
            z = (z + k) % 4
        else:
            y = (y + k) % 4
        pairs.append((device, (4 * y + z) * 8 + 2 * x + core))
    return pairs


def send(value, kind, k):
    return lax.ppermute(value, AXES, shifted(kind, k))


def cross(a, b, precision=None):
    return lax.dot_general(
        a, b, (((0,), (0,)), ((), ())), precision=precision, preferred_element_type=jnp.float32
    )


def halves(value):
    hi = value.astype(jnp.bfloat16)
    return hi, (value - hi.astype(jnp.float32)).astype(jnp.bfloat16)


def gram_of_few(value, columns):
    hi, lo = halves(value)
    left = jnp.concatenate([hi, hi, lo], axis=0)
    right = jnp.concatenate([hi, lo, hi], axis=0)
    return cross(left[:, columns], right[:, columns.start :])


def gram_kernel(x_hbm, *refs):
    outs, (x, halved, top, low, shift, total, packed, loads) = refs[:4], refs[4:]
    chunks = DEMES // CHUNK

    def load(n):
        part = pl.ds(n * CHUNK, CHUNK)
        return pltpu.make_async_copy(x_hbm.at[part], x.at[part], loads.at[n])

    def split(n, to):
        d = x[pl.ds(n * CHUNK, CHUNK)] - shift[...][None]
        total[...] += jnp.sum(d, axis=0)
        to[:, LOCI:], to[:, :LOCI] = halves(d.reshape(CHUNK * GENS, LOCI))

    def multiply(part):
        top_part = cross(part[:, :768], part[:, 512:768])
        low_part = cross(part[...], part[:, 768:])
        top[...] += top_part
        low[...] += low_part

    for n in range(chunks):
        load(n).start()
    total[...] = jnp.zeros_like(total)
    top[...] = jnp.zeros_like(top)
    low[...] = jnp.zeros_like(low)
    load(0).wait()
    shift[...] = jnp.sum(x[:CHUNK], axis=0) * (1.0 / CHUNK)
    split(0, halved)
    multiply(halved)

    def body(n, carry):
        load(n).wait()
        split(n, halved)
        multiply(halved)
        return carry

    lax.fori_loop(1, chunks, body, 0)

    sums = total[...]

    def part(first_row, i, j):
        rows = slice(first_row + BLOCK * i, first_row + BLOCK * (i + 1))
        if j < 2:
            return top[rows, BLOCK * j : BLOCK * (j + 1)]
        return low[rows, BLOCK * (j - 2) : BLOCK * (j - 1)]

    for i in range(4):
        offset = gram_of_few(sums, slice(BLOCK * i, BLOCK * (i + 1))) * (1.0 / DEMES)
        for j in range(i, 4):
            n = PAIRS.index((i, j))
            block = part(LOCI, i, j) + (part(0, i, j) + part(0, j, i).T)
            packed[BLOCK * n : BLOCK * (n + 1), :] = block - offset[:, BLOCK * (j - i) : BLOCK * (j - i + 1)]
    mean = shift[...] + sums * (1.0 / DEMES)
    first, second, core = place()
    for k, out in enumerate(outs):
        to = (first + k) % 4
        for j in range(4):
            row = pl.multiple_of(piece_row(core, to, j), 8)
            out[PIECE * j : PIECE * (j + 1), :] = packed[pl.ds(row, PIECE), :]
            out[4 * PIECE + 32 * j : 4 * PIECE + 32 * (j + 1), :] = mean[:, BLOCK * j : BLOCK * (j + 1)]


def local_gram(freqs):
    rows = 4 * PIECE + MEAN_ROWS
    return pl.pallas_call(
        gram_kernel,
        in_specs=[pl.BlockSpec(memory_space=pltpu.HBM)],
        out_specs=[pl.BlockSpec(memory_space=pltpu.VMEM)] * 4,
        out_shape=[jax.ShapeDtypeStruct((rows, BLOCK), jnp.float32)] * 4,
        scratch_shapes=[
            pltpu.VMEM((DEMES, GENS, LOCI), jnp.float32),
            pltpu.VMEM((CHUNK * GENS, 2 * LOCI), jnp.bfloat16),
            pltpu.VMEM((768, 256), jnp.float32),
            pltpu.VMEM((1024, 256), jnp.float32),
            pltpu.VMEM((GENS, LOCI), jnp.float32),
            pltpu.VMEM((GENS, LOCI), jnp.float32),
            pltpu.VMEM((PACKED, BLOCK), jnp.float32),
            pltpu.SemaphoreType.DMA((DEMES // CHUNK,)),
        ],
        compiler_params=pltpu.CompilerParams(vmem_limit_bytes=48 * MIB),
        name="local_gram",
    )(freqs)


def merge(refs, rows, weight, packed):
    wide = [
        jnp.concatenate([ref[rows + 32 * j : rows + 32 * (j + 1), :] for j in range(4)], axis=1) for ref in refs
    ]
    mean = ((wide[0] + wide[2]) + (wide[1] + wide[3])) * 0.25
    delta = jnp.concatenate([part - mean for part in wide], axis=0)
    for i in range(4):
        product = gram_of_few(delta, slice(BLOCK * i, BLOCK * (i + 1)))
        for j in range(i, 4):
            n = PAIRS.index((i, j))
            packed[BLOCK * n : BLOCK * (n + 1), :] = product[:, BLOCK * (j - i) : BLOCK * (j - i + 1)] * weight
    return mean


def first_kernel(*refs):
    ins, outs, (packed, summed) = refs[:4], refs[4:8], refs[8:]
    mean = merge(ins, 4 * PIECE, float(DEMES), packed)
    first, second, core = place()
    for j in range(4):
        rows = slice(PIECE * j, PIECE * (j + 1))
        row = pl.multiple_of(piece_row(core, first, j), 8)
        summed[rows, :] = ((ins[0][rows, :] + ins[2][rows, :]) + (ins[1][rows, :] + ins[3][rows, :])) + packed[
            pl.ds(row, PIECE), :
        ]
    for k, out in enumerate(outs):
        row = pl.multiple_of(PIECE * ((second + k) % 4), 8)
        out[:PIECE, :] = summed[pl.ds(row, PIECE), :]
        for j in range(4):
            out[PIECE + 32 * j : PIECE + 32 * (j + 1), :] = mean[:, BLOCK * j : BLOCK * (j + 1)]


def second_kernel(*refs):
    ins, (out, mean_out), (packed,) = refs[:4], refs[4:6], refs[6:]
    mean_out[...] = merge(ins, PIECE, 4.0 * DEMES, packed)
    first, second, core = place()
    row = pl.multiple_of(piece_row(core, first, second), 8)
    rows = slice(0, PIECE)
    out[...] = ((ins[0][rows, :] + ins[2][rows, :]) + (ins[1][rows, :] + ins[3][rows, :])) + packed[
        pl.ds(row, PIECE), :
    ]


def merge_first(parts):
    rows = PIECE + MEAN_ROWS
    return pl.pallas_call(
        first_kernel,
        out_shape=[jax.ShapeDtypeStruct((rows, BLOCK), jnp.float32)] * 4,
        scratch_shapes=[pltpu.VMEM((PACKED, BLOCK), jnp.float32), pltpu.VMEM((4 * PIECE, BLOCK), jnp.float32)],
        compiler_params=pltpu.CompilerParams(vmem_limit_bytes=16 * MIB),
        name="merge_first",
    )(*parts)


def merge_second(parts):
    return pl.pallas_call(
        second_kernel,
        out_shape=[
            jax.ShapeDtypeStruct((PIECE, BLOCK), jnp.float32),
            jax.ShapeDtypeStruct((GENS, LOCI), jnp.float32),
        ],
        scratch_shapes=[pltpu.VMEM((PACKED, BLOCK), jnp.float32)],
        compiler_params=pltpu.CompilerParams(vmem_limit_bytes=16 * MIB),
        name="merge_second",
    )(*parts)


def inverse_cholesky(s):
    full = (8, RANK)
    lane = lax.broadcasted_iota(jnp.int32, full, 1)
    sub = lax.broadcasted_iota(jnp.int32, full, 0)
    count = RANK // 8
    rows = [s[8 * i : 8 * i + 8, :] for i in range(count)]

    def spread_row(value, j):
        return jnp.broadcast_to(value[j : j + 1, :], full)

    def spread_columns(i, k):
        return [jnp.broadcast_to(rows[i][:, 8 * k + j : 8 * k + j + 1], full) for j in range(8)]

    own_columns = spread_columns(0, 0)
    for k in range(count):
        here = (lane >= 8 * k) & (lane < 8 * k + 8)
        own = jnp.where(here, jnp.where(lane - 8 * k == sub, 1.0, 0.0), rows[k])
        last = k == count - 1
        if not last:
            near = spread_columns(k + 1, k)
            after = spread_columns(k + 1, k + 1)
            near_rows = jnp.where(here, 0.0, rows[k + 1])
        ratio, scaled, scale = {}, [], None
        for j in range(8):
            inverse = 1.0 / spread_row(own_columns[j], j)
            for l in range(j + 1, 8):
                ratio[l, j] = spread_row(own_columns[j], l) * inverse
                own_columns[l] = own_columns[l] - own_columns[j] * ratio[l, j]
            scaled.append(spread_row(own, j) * inverse)
            if j < 7:
                own = own - jnp.where(sub > j, own_columns[j], 0.0) * scaled[j]
            scale = jnp.where(sub == j, inverse, scale) if j else inverse
            if not last:
                near_rows = near_rows - near[j] * scaled[j]
                for l in range(8):
                    after[l] = after[l] - near[j] * (spread_row(near[j], l) * inverse)
                for l in range(j + 1, 8):
                    near[l] = near[l] - near[j] * ratio[l, j]
        solved = list(scaled)
        for j in range(7, 0, -1):
            for m in range(j):
                solved[m] = solved[m] - ratio[j, m] * solved[j]
        for i in range(k + 2, count):
            t = [column * part for column, part in zip(spread_columns(i, k), solved)]
            rows[i] = jnp.where(here, 0.0, rows[i]) - (
                ((t[0] + t[1]) + (t[2] + t[3])) + ((t[4] + t[5]) + (t[6] + t[7]))
            )
        rows[k] = jnp.where(lane <= 8 * k + sub, own * jnp.sqrt(scale), 0.0)
        if not last:
            rows[k + 1] = near_rows
            own_columns = after
    return jnp.concatenate(rows, axis=0)


STEP = 16
STEPS = DEMES // STEP
LOADS = 4


def core_kernel(
    p0, p1, p2, p3, start_ref, mean_ref, x_hbm, core_hbm, factor_ref,
    x, core, packed, gram, both, hi_a, lo_a, hi_b, lo_b, loads, stores,
):
    def load(n):
        part = pl.ds(n * (DEMES // LOADS), DEMES // LOADS)
        return pltpu.make_async_copy(x_hbm.at[part], x.at[part], loads.at[n])

    def store(n):
        part = pl.ds(n * STEP, STEP)
        return pltpu.make_async_copy(core.at[part], core_hbm.at[part], stores.at[n])

    for n in range(LOADS):
        load(n).start()

    first, second, core_id = place()
    for k, part in enumerate((p0, p1, p2, p3)):
        for l in range(4):
            row = pl.multiple_of(piece_row(core_id, (first + 4 - k) % 4, (second + 4 - l) % 4), 8)
            packed[pl.ds(row, PIECE), :] = part[PIECE * l : PIECE * (l + 1), :]
    for n, (i, j) in enumerate(PAIRS):
        block = packed[BLOCK * n : BLOCK * (n + 1), :] * (1.0 / (4096 * 256))
        gram[BLOCK * i : BLOCK * (i + 1), BLOCK * j : BLOCK * (j + 1)] = block
        if i != j:
            gram[BLOCK * j : BLOCK * (j + 1), BLOCK * i : BLOCK * (i + 1)] = block.T

    def body(_, basis):
        z = jnp.dot(basis, gram[...], precision=lax.Precision.HIGHEST, preferred_element_type=jnp.float32)
        small = lax.dot_general(
            z, z, (((1,), (1,)), ((), ())), precision=lax.Precision.HIGHEST, preferred_element_type=jnp.float32
        )
        return jnp.dot(
            inverse_cholesky(small), z, precision=lax.Precision.HIGHEST, preferred_element_type=jnp.float32
        )

    basis = lax.fori_loop(0, ITERS, body, start_ref[...].T)
    factor = basis.T
    factor_ref[...] = factor
    hi = factor.astype(jnp.bfloat16)
    both[:, :RANK] = hi
    both[:, RANK:] = (factor - hi.astype(jnp.float32)).astype(jnp.bfloat16)
    for n in range(LOADS):
        load(n).wait()

    def split(n, d_hi, d_lo):
        d = (x[pl.ds(n * STEP, STEP)] - mean_ref[...][None]).reshape(STEP * GENS, LOCI)
        d_hi[...] = d.astype(jnp.bfloat16)
        d_lo[...] = (d - d.astype(jnp.bfloat16).astype(jnp.float32)).astype(jnp.bfloat16)

    def multiply(n, d_hi, d_lo):
        wide = jnp.dot(d_hi[...], both[...], preferred_element_type=jnp.float32)
        rest = jnp.dot(d_lo[...], both[:, :RANK], preferred_element_type=jnp.float32)
        core[pl.ds(n * STEP, STEP)] = (wide[:, :RANK] + (wide[:, RANK:] + rest)).reshape(STEP, GENS, RANK)

    def pair(p, carry):
        split(2 * p + 1, hi_b, lo_b)
        multiply(2 * p, hi_a, lo_a)
        split(jnp.minimum(2 * p + 2, STEPS - 1), hi_a, lo_a)
        multiply(2 * p + 1, hi_b, lo_b)
        store(2 * p).start()
        store(2 * p + 1).start()
        return carry

    split(0, hi_a, lo_a)
    lax.fori_loop(0, STEPS // 2, pair, 0)
    for n in range(STEPS):
        store(n).wait()


def iterate(parts, start_basis, mean, freqs):
    vmem = pl.BlockSpec(memory_space=pltpu.VMEM)
    hbm = pl.BlockSpec(memory_space=pltpu.HBM)
    return pl.pallas_call(
        core_kernel,
        in_specs=[vmem] * 6 + [hbm],
        out_specs=[hbm, vmem],
        out_shape=[
            jax.ShapeDtypeStruct((DEMES, GENS, RANK), jnp.float32),
            jax.ShapeDtypeStruct((LOCI, RANK), jnp.float32),
        ],
        scratch_shapes=[
            pltpu.VMEM((DEMES, GENS, LOCI), jnp.float32),
            pltpu.VMEM((DEMES, GENS, RANK), jnp.float32),
            pltpu.VMEM((PACKED, BLOCK), jnp.float32),
            pltpu.VMEM((LOCI, LOCI), jnp.float32),
            pltpu.VMEM((LOCI, 2 * RANK), jnp.bfloat16),
        ]
        + [pltpu.VMEM((STEP * GENS, LOCI), jnp.bfloat16)] * 4
        + [
            pltpu.SemaphoreType.DMA((LOADS,)),
            pltpu.SemaphoreType.DMA((STEPS,)),
        ],
        compiler_params=pltpu.CompilerParams(vmem_limit_bytes=48 * MIB),
        name="iterate",
    )(*parts, start_basis, mean, freqs)


def local(freqs, start_basis):
    out = local_gram(freqs)
    parts = merge_first([out[0]] + [send(out[k], "first", k) for k in (1, 2, 3)])
    shard, mean = merge_second([parts[0]] + [send(parts[k], "second", k) for k in (1, 2, 3)])
    one, two, three = [send(shard, "x", k) for k in (1, 2, 3)]
    shard = (shard + two) + (one + three)
    shard = shard + send(shard, "core", 1)
    row = jnp.concatenate([shard] + [send(shard, "second", k) for k in (1, 2, 3)], axis=0)
    rows = [row] + [send(row, "first", k) for k in (1, 2, 3)]
    return tuple(iterate(rows, start_basis, mean, freqs))


def solution(mesh):
    in_specs = (P("deme", "gen", None), P())
    out_specs = (P("deme", "gen", None), P())
    return jax.shard_map(local, mesh=mesh, in_specs=in_specs, out_specs=out_specs, check_vma=False)
```

```python
import jax
import jax.numpy as jnp
from jax import lax
from jax.experimental import pallas as pl
from jax.experimental.pallas import tpu as pltpu
from jax.sharding import PartitionSpec as P

ITERS = 4
LOCI = 512
RANK = 128
BLOCK = 128
PIECE = 80
PACKED = 1280
PAIRS = [(i, j) for i in range(4) for j in range(i, 4)]
DEMES = 256
GENS = 32
CHUNK = 32
MEAN_ROWS = 128
AXES = ("deme", "gen")
MIB = 1024 * 1024


def place():
    deme, gen = lax.axis_index("deme"), lax.axis_index("gen")
    y, z, core = deme // 4, deme % 4, gen % 2
    return jnp.where(core == 0, z, y), jnp.where(core == 0, y, z), core


def piece_row(core, first, second):
    return PIECE * jnp.where(core == 0, 4 * first + second, 4 * second + first)


def shifted(kind, k):
    pairs = []
    for device in range(128):
        deme, gen = divmod(device, 8)
        y, z = divmod(deme, 4)
        x, core = divmod(gen, 2)
        if kind == "x":
            x = (x + k) % 4
        elif kind == "core":
            core = 1 - core
        elif (kind == "first") == (core == 0):
            z = (z + k) % 4
        else:
            y = (y + k) % 4
        pairs.append((device, (4 * y + z) * 8 + 2 * x + core))
    return pairs


def send(value, kind, k):
    return lax.ppermute(value, AXES, shifted(kind, k))


def cross(a, b, precision=None):
    return lax.dot_general(
        a, b, (((0,), (0,)), ((), ())), precision=precision, preferred_element_type=jnp.float32
    )


def halves(value):
    hi = value.astype(jnp.bfloat16)
    return hi, (value - hi.astype(jnp.float32)).astype(jnp.bfloat16)


def gram_of_few(value, columns):
    hi, lo = halves(value)
    left = jnp.concatenate([hi, hi, lo], axis=0)
    right = jnp.concatenate([hi, lo, hi], axis=0)
    return cross(left[:, columns], right[:, columns.start :])


def gram_kernel(x_hbm, *refs):
    outs, (x, halved, top, low, shift, total, packed, loads) = refs[:4], refs[4:]
    chunks = DEMES // CHUNK

    def load(n):
        part = pl.ds(n * CHUNK, CHUNK)
        return pltpu.make_async_copy(x_hbm.at[part], x.at[part], loads.at[n])

    def split(n, to):
        d = x[pl.ds(n * CHUNK, CHUNK)] - shift[...][None]
        total[...] += jnp.sum(d, axis=0)
        to[:, LOCI:], to[:, :LOCI] = halves(d.reshape(CHUNK * GENS, LOCI))

    def multiply(part):
        top_part = cross(part[:, :768], part[:, 512:768])
        low_part = cross(part[...], part[:, 768:])
        top[...] += top_part
        low[...] += low_part

    for n in range(chunks):
        load(n).start()
    total[...] = jnp.zeros_like(total)
    top[...] = jnp.zeros_like(top)
    low[...] = jnp.zeros_like(low)
    load(0).wait()
    shift[...] = jnp.sum(x[:CHUNK], axis=0) * (1.0 / CHUNK)
    split(0, halved)
    multiply(halved)

    def body(n, carry):
        load(n).wait()
        split(n, halved)
        multiply(halved)
        return carry

    lax.fori_loop(1, chunks, body, 0)

    sums = total[...]

    def part(first_row, i, j):
        rows = slice(first_row + BLOCK * i, first_row + BLOCK * (i + 1))
        if j < 2:
            return top[rows, BLOCK * j : BLOCK * (j + 1)]
        return low[rows, BLOCK * (j - 2) : BLOCK * (j - 1)]

    for i in range(4):
        offset = gram_of_few(sums, slice(BLOCK * i, BLOCK * (i + 1))) * (1.0 / DEMES)
        for j in range(i, 4):
            n = PAIRS.index((i, j))
            block = part(LOCI, i, j) + (part(0, i, j) + part(0, j, i).T)
            packed[BLOCK * n : BLOCK * (n + 1), :] = block - offset[:, BLOCK * (j - i) : BLOCK * (j - i + 1)]
    mean = shift[...] + sums * (1.0 / DEMES)
    first, second, core = place()
    for k, out in enumerate(outs):
        to = (first + k) % 4
        for j in range(4):
            row = pl.multiple_of(piece_row(core, to, j), 8)
            out[PIECE * j : PIECE * (j + 1), :] = packed[pl.ds(row, PIECE), :]
            out[4 * PIECE + 32 * j : 4 * PIECE + 32 * (j + 1), :] = mean[:, BLOCK * j : BLOCK * (j + 1)]


def local_gram(freqs):
    rows = 4 * PIECE + MEAN_ROWS
    return pl.pallas_call(
        gram_kernel,
        in_specs=[pl.BlockSpec(memory_space=pltpu.HBM)],
        out_specs=[pl.BlockSpec(memory_space=pltpu.VMEM)] * 4,
        out_shape=[jax.ShapeDtypeStruct((rows, BLOCK), jnp.float32)] * 4,
        scratch_shapes=[
            pltpu.VMEM((DEMES, GENS, LOCI), jnp.float32),
            pltpu.VMEM((CHUNK * GENS, 2 * LOCI), jnp.bfloat16),
            pltpu.VMEM((768, 256), jnp.float32),
            pltpu.VMEM((1024, 256), jnp.float32),
            pltpu.VMEM((GENS, LOCI), jnp.float32),
            pltpu.VMEM((GENS, LOCI), jnp.float32),
            pltpu.VMEM((PACKED, BLOCK), jnp.float32),
            pltpu.SemaphoreType.DMA((DEMES // CHUNK,)),
        ],
        compiler_params=pltpu.CompilerParams(vmem_limit_bytes=48 * MIB),
        name="local_gram",
    )(freqs)


def merge(refs, index, weight, packed, delta):
    rows = 4 * PIECE
    wide = [
        jnp.concatenate([ref[rows + 32 * j : rows + 32 * (j + 1), :] for j in range(4)], axis=1) for ref in refs
    ]
    mean = ((wide[0] + wide[2]) + (wide[1] + wide[3])) * 0.25
    for k, part in enumerate(wide):
        delta[pl.ds(pl.multiple_of(GENS * ((index + 4 - k) % 4), GENS), GENS), :] = part - mean
    for i in range(4):
        product = gram_of_few(delta[...], slice(BLOCK * i, BLOCK * (i + 1)))
        for j in range(i, 4):
            n = PAIRS.index((i, j))
            packed[BLOCK * n : BLOCK * (n + 1), :] = product[:, BLOCK * (j - i) : BLOCK * (j - i + 1)] * weight
    return mean


def merged_rows(refs, first, core, packed, out):
    for j in range(4):
        rows = slice(PIECE * j, PIECE * (j + 1))
        row = pl.multiple_of(piece_row(core, first, j), 8)
        out[rows, :] = ((refs[0][rows, :] + refs[2][rows, :]) + (refs[1][rows, :] + refs[3][rows, :])) + packed[
            pl.ds(row, PIECE), :
        ]


def first_kernel(*refs):
    ins, out, (packed, delta) = refs[:4], refs[4], refs[5:]
    first, second, core = place()
    mean = merge(ins, first, float(DEMES), packed, delta)
    merged_rows(ins, first, core, packed, out)
    for j in range(4):
        out[4 * PIECE + 32 * j : 4 * PIECE + 32 * (j + 1), :] = mean[:, BLOCK * j : BLOCK * (j + 1)]


def second_kernel(*refs):
    ins, (out, mean_out), (packed, delta) = refs[:4], refs[4:6], refs[6:]
    first, second, core = place()
    mean_out[...] = merge(ins, second, 4.0 * DEMES, packed, delta)
    merged_rows(ins, first, core, packed, out)


MERGE_SCRATCH = [pltpu.VMEM((PACKED, BLOCK), jnp.float32), pltpu.VMEM((4 * GENS, LOCI), jnp.float32)]


def merge_first(parts):
    return pl.pallas_call(
        first_kernel,
        out_shape=jax.ShapeDtypeStruct((4 * PIECE + MEAN_ROWS, BLOCK), jnp.float32),
        scratch_shapes=MERGE_SCRATCH,
        compiler_params=pltpu.CompilerParams(vmem_limit_bytes=16 * MIB),
        name="merge_first",
    )(*parts)


def merge_second(parts):
    return pl.pallas_call(
        second_kernel,
        out_shape=[
            jax.ShapeDtypeStruct((4 * PIECE, BLOCK), jnp.float32),
            jax.ShapeDtypeStruct((GENS, LOCI), jnp.float32),
        ],
        scratch_shapes=MERGE_SCRATCH,
        compiler_params=pltpu.CompilerParams(vmem_limit_bytes=16 * MIB),
        name="merge_second",
    )(*parts)


def inverse_cholesky(s):
    full = (8, RANK)
    lane = lax.broadcasted_iota(jnp.int32, full, 1)
    sub = lax.broadcasted_iota(jnp.int32, full, 0)
    count = RANK // 8
    rows = [s[8 * i : 8 * i + 8, :] for i in range(count)]

    def spread_row(value, j):
        return jnp.broadcast_to(value[j : j + 1, :], full)

    def spread_columns(i, k):
        return [jnp.broadcast_to(rows[i][:, 8 * k + j : 8 * k + j + 1], full) for j in range(8)]

    own_columns = spread_columns(0, 0)
    for k in range(count):
        here = (lane >= 8 * k) & (lane < 8 * k + 8)
        own = jnp.where(here, jnp.where(lane - 8 * k == sub, 1.0, 0.0), rows[k])
        last = k == count - 1
        if not last:
            near = spread_columns(k + 1, k)
            after = spread_columns(k + 1, k + 1)
            near_rows = jnp.where(here, 0.0, rows[k + 1])
        ratio, scaled, scale = {}, [], None
        for j in range(8):
            inverse = 1.0 / spread_row(own_columns[j], j)
            for l in range(j + 1, 8):
                ratio[l, j] = spread_row(own_columns[j], l) * inverse
                own_columns[l] = own_columns[l] - own_columns[j] * ratio[l, j]
            scaled.append(spread_row(own, j) * inverse)
            if j < 7:
                own = own - jnp.where(sub > j, own_columns[j], 0.0) * scaled[j]
            scale = jnp.where(sub == j, inverse, scale) if j else inverse
            if not last:
                near_rows = near_rows - near[j] * scaled[j]
                for l in range(8):
                    after[l] = after[l] - near[j] * (spread_row(near[j], l) * inverse)
                for l in range(j + 1, 8):
                    near[l] = near[l] - near[j] * ratio[l, j]
        solved = list(scaled)
        for j in range(7, 0, -1):
            for m in range(j):
                solved[m] = solved[m] - ratio[j, m] * solved[j]
        for i in range(k + 2, count):
            t = [column * part for column, part in zip(spread_columns(i, k), solved)]
            rows[i] = jnp.where(here, 0.0, rows[i]) - (
                ((t[0] + t[1]) + (t[2] + t[3])) + ((t[4] + t[5]) + (t[6] + t[7]))
            )
        rows[k] = jnp.where(lane <= 8 * k + sub, own * jnp.sqrt(scale), 0.0)
        if not last:
            rows[k + 1] = near_rows
            own_columns = after
    return jnp.concatenate(rows, axis=0)


def thirds(value):
    one = value.astype(jnp.bfloat16)
    value = value - one.astype(jnp.float32)
    two = value.astype(jnp.bfloat16)
    return one, two, (value - two.astype(jnp.float32)).astype(jnp.bfloat16)


def plain(a, b):
    return jnp.dot(a, b, preferred_element_type=jnp.float32)


def rows_product(a, b):
    return lax.dot_general(a, b, (((1,), (1,)), ((), ())), preferred_element_type=jnp.float32)


STEP = 16
STEPS = DEMES // STEP
LOADS = 4


def core_kernel(
    p0, p1, p2, p3, q0, q1, q2, q3, start_ref, mean_ref, x_hbm, core_hbm, factor_ref,
    x, core, packed, gram, gram_1, gram_2, gram_3, both, hi_a, lo_a, hi_b, lo_b, loads, stores,
):
    def load(n):
        part = pl.ds(n * (DEMES // LOADS), DEMES // LOADS)
        return pltpu.make_async_copy(x_hbm.at[part], x.at[part], loads.at[n])

    def store(n):
        part = pl.ds(n * STEP, STEP)
        return pltpu.make_async_copy(core.at[part], core_hbm.at[part], stores.at[n])

    for n in range(LOADS):
        load(n).start()

    first, second, core_id = place()
    for k, part in enumerate((p0, p1, p2, p3)):
        for l in range(4):
            row = pl.multiple_of(piece_row(core_id, (first + 4 - k) % 4, l), 8)
            packed[pl.ds(row, PIECE), :] = part[PIECE * l : PIECE * (l + 1), :]
    for k, part in enumerate((q0, q1, q2, q3)):
        for l in range(4):
            row = pl.multiple_of(piece_row(1 - core_id, (second + 4 - k) % 4, l), 8)
            packed[pl.ds(row, PIECE), :] += part[PIECE * l : PIECE * (l + 1), :]
    for n, (i, j) in enumerate(PAIRS):
        block = packed[BLOCK * n : BLOCK * (n + 1), :] * (1.0 / (4096 * 256))
        gram[BLOCK * i : BLOCK * (i + 1), BLOCK * j : BLOCK * (j + 1)] = block
        if i != j:
            gram[BLOCK * j : BLOCK * (j + 1), BLOCK * i : BLOCK * (i + 1)] = block.T

    gram_1[...], gram_2[...], gram_3[...] = thirds(gram[...])

    def body(_, basis):
        one, two, three = thirds(basis)
        by_first = plain(jnp.concatenate([one, two, three], axis=0), gram_1[...])
        by_second = plain(jnp.concatenate([one, two], axis=0), gram_2[...])
        z = by_first[:RANK] + (
            (by_first[RANK : 2 * RANK] + by_second[:RANK])
            + ((by_first[2 * RANK :] + by_second[RANK:]) + plain(one, gram_3[...]))
        )
        one, two, three = thirds(z)
        wide = rows_product(jnp.concatenate([one, two, three], axis=0), jnp.concatenate([one, two], axis=0))
        small = wide[:RANK, :RANK] + (
            (wide[RANK : 2 * RANK, :RANK] + wide[:RANK, RANK:])
            + ((wide[2 * RANK :, :RANK] + rows_product(one, three)) + wide[RANK : 2 * RANK, RANK:])
        )
        w_one, w_two, w_three = thirds(inverse_cholesky(small))
        w_pair = jnp.concatenate([w_one, w_two], axis=1)
        large = plain(w_pair, jnp.concatenate([one, one], axis=0))
        middle = plain(w_pair, jnp.concatenate([two, two], axis=0))
        rest = plain(jnp.concatenate([w_one, w_three], axis=1), jnp.concatenate([three, one], axis=0))
        return large + (middle + rest)

    basis = lax.fori_loop(0, ITERS, body, start_ref[...].T)
    factor = basis.T
    factor_ref[...] = factor
    hi = factor.astype(jnp.bfloat16)
    both[:, :RANK] = hi
    both[:, RANK:] = (factor - hi.astype(jnp.float32)).astype(jnp.bfloat16)
    for n in range(LOADS):
        load(n).wait()

    def split(n, d_hi, d_lo):
        d = (x[pl.ds(n * STEP, STEP)] - mean_ref[...][None]).reshape(STEP * GENS, LOCI)
        d_hi[...] = d.astype(jnp.bfloat16)
        d_lo[...] = (d - d.astype(jnp.bfloat16).astype(jnp.float32)).astype(jnp.bfloat16)

    def multiply(n, d_hi, d_lo):
        wide = jnp.dot(d_hi[...], both[...], preferred_element_type=jnp.float32)
        rest = jnp.dot(d_lo[...], both[:, :RANK], preferred_element_type=jnp.float32)
        core[pl.ds(n * STEP, STEP)] = (wide[:, :RANK] + (wide[:, RANK:] + rest)).reshape(STEP, GENS, RANK)

    def pair(p, carry):
        split(2 * p + 1, hi_b, lo_b)
        multiply(2 * p, hi_a, lo_a)
        split(jnp.minimum(2 * p + 2, STEPS - 1), hi_a, lo_a)
        multiply(2 * p + 1, hi_b, lo_b)
        store(2 * p).start()
        store(2 * p + 1).start()
        return carry

    split(0, hi_a, lo_a)
    lax.fori_loop(0, STEPS // 2, pair, 0, unroll=2)
    for n in range(STEPS):
        store(n).wait()


def iterate(parts, start_basis, mean, freqs):
    vmem = pl.BlockSpec(memory_space=pltpu.VMEM)
    hbm = pl.BlockSpec(memory_space=pltpu.HBM)
    return pl.pallas_call(
        core_kernel,
        in_specs=[vmem] * 10 + [hbm],
        out_specs=[hbm, vmem],
        out_shape=[
            jax.ShapeDtypeStruct((DEMES, GENS, RANK), jnp.float32),
            jax.ShapeDtypeStruct((LOCI, RANK), jnp.float32),
        ],
        scratch_shapes=[
            pltpu.VMEM((DEMES, GENS, LOCI), jnp.float32),
            pltpu.VMEM((DEMES, GENS, RANK), jnp.float32),
            pltpu.VMEM((PACKED, BLOCK), jnp.float32),
            pltpu.VMEM((LOCI, LOCI), jnp.float32),
            pltpu.VMEM((LOCI, LOCI), jnp.bfloat16),
            pltpu.VMEM((LOCI, LOCI), jnp.bfloat16),
            pltpu.VMEM((LOCI, LOCI), jnp.bfloat16),
            pltpu.VMEM((LOCI, 2 * RANK), jnp.bfloat16),
        ]
        + [pltpu.VMEM((STEP * GENS, LOCI), jnp.bfloat16)] * 4
        + [
            pltpu.SemaphoreType.DMA((LOADS,)),
            pltpu.SemaphoreType.DMA((STEPS,)),
        ],
        compiler_params=pltpu.CompilerParams(vmem_limit_bytes=48 * MIB),
        name="iterate",
    )(*parts, start_basis, mean, freqs)


def local(freqs, start_basis):
    out = local_gram(freqs)
    rows = merge_first([out[0]] + [send(out[k], "first", k) for k in (1, 2, 3)])
    rows, mean = merge_second([rows] + [send(rows, "second", k) for k in (1, 2, 3)])
    one, two, three = [send(rows, "x", k) for k in (1, 2, 3)]
    rows = (rows + two) + (one + three)
    parts = [rows] + [send(rows, "first", k) for k in (1, 2, 3)]
    parts += [send(part, "core", 1) for part in parts]
    return tuple(iterate(parts, start_basis, mean, freqs))


def solution(mesh):
    in_specs = (P("deme", "gen", None), P())
    out_specs = (P("deme", "gen", None), P())
    return jax.shard_map(local, mesh=mesh, in_specs=in_specs, out_specs=out_specs, check_vma=False)
```

```python
import jax
import jax.numpy as jnp
from jax import lax
from jax.experimental import pallas as pl
from jax.experimental.pallas import tpu as pltpu
from jax.sharding import PartitionSpec as P

ITERS = 4
LOCI = 512
RANK = 128
BLOCK = 128
PIECE = 80
PACKED = 1280
PAIRS = [(i, j) for i in range(4) for j in range(i, 4)]
DEMES = 256
GENS = 32
CHUNK = 32
MEAN_ROWS = 128
AXES = ("deme", "gen")
MIB = 1024 * 1024


def place():
    deme, gen = lax.axis_index("deme"), lax.axis_index("gen")
    y, z, core = deme // 4, deme % 4, gen % 2
    return jnp.where(core == 0, z, y), jnp.where(core == 0, y, z), core


def piece_row(core, first, second):
    return PIECE * jnp.where(core == 0, 4 * first + second, 4 * second + first)


def shifted(kind, k):
    pairs = []
    for device in range(128):
        deme, gen = divmod(device, 8)
        y, z = divmod(deme, 4)
        x, core = divmod(gen, 2)
        if kind == "x":
            x = (x + k) % 4
        elif kind == "core":
            core = 1 - core
        elif (kind == "first") == (core == 0):
            z = (z + k) % 4
        else:
            y = (y + k) % 4
        pairs.append((device, (4 * y + z) * 8 + 2 * x + core))
    return pairs


def send(value, kind, k):
    return lax.ppermute(value, AXES, shifted(kind, k))


def cross(a, b, precision=None):
    return lax.dot_general(
        a, b, (((0,), (0,)), ((), ())), precision=precision, preferred_element_type=jnp.float32
    )


def halves(value):
    hi = value.astype(jnp.bfloat16)
    return hi, (value - hi.astype(jnp.float32)).astype(jnp.bfloat16)


def gram_of_few(value, columns):
    hi, lo = halves(value)
    left = jnp.concatenate([hi, hi, lo], axis=0)
    right = jnp.concatenate([hi, lo, hi], axis=0)
    return cross(left[:, columns], right[:, columns.start :])


def gram_kernel(x_hbm, *refs):
    outs, (x, halved, top, low, shift, total, packed, loads) = refs[:4], refs[4:]
    chunks = DEMES // CHUNK

    def load(n):
        part = pl.ds(n * CHUNK, CHUNK)
        return pltpu.make_async_copy(x_hbm.at[part], x.at[part], loads.at[n])

    def split(n, to):
        d = x[pl.ds(n * CHUNK, CHUNK)] - shift[...][None]
        total[...] += jnp.sum(d, axis=0)
        to[:, LOCI:], to[:, :LOCI] = halves(d.reshape(CHUNK * GENS, LOCI))

    def multiply(part):
        top_part = cross(part[:, :768], part[:, 512:768])
        low_part = cross(part[...], part[:, 768:])
        top[...] += top_part
        low[...] += low_part

    for n in range(chunks):
        load(n).start()
    total[...] = jnp.zeros_like(total)
    top[...] = jnp.zeros_like(top)
    low[...] = jnp.zeros_like(low)
    load(0).wait()
    shift[...] = jnp.sum(x[:CHUNK], axis=0) * (1.0 / CHUNK)
    split(0, halved)
    multiply(halved)

    def body(n, carry):
        load(n).wait()
        split(n, halved)
        multiply(halved)
        return carry

    lax.fori_loop(1, chunks, body, 0)

    sums = total[...]

    def part(first_row, i, j):
        rows = slice(first_row + BLOCK * i, first_row + BLOCK * (i + 1))
        if j < 2:
            return top[rows, BLOCK * j : BLOCK * (j + 1)]
        return low[rows, BLOCK * (j - 2) : BLOCK * (j - 1)]

    for i in range(4):
        offset = gram_of_few(sums, slice(BLOCK * i, BLOCK * (i + 1))) * (1.0 / DEMES)
        for j in range(i, 4):
            n = PAIRS.index((i, j))
            block = part(LOCI, i, j) + (part(0, i, j) + part(0, j, i).T)
            packed[BLOCK * n : BLOCK * (n + 1), :] = block - offset[:, BLOCK * (j - i) : BLOCK * (j - i + 1)]
    mean = shift[...] + sums * (1.0 / DEMES)
    first, second, core = place()
    for k, out in enumerate(outs):
        to = (first + k) % 4
        for j in range(4):
            row = pl.multiple_of(piece_row(core, to, j), 8)
            out[PIECE * j : PIECE * (j + 1), :] = packed[pl.ds(row, PIECE), :]
            out[4 * PIECE + 32 * j : 4 * PIECE + 32 * (j + 1), :] = mean[:, BLOCK * j : BLOCK * (j + 1)]


def local_gram(freqs):
    rows = 4 * PIECE + MEAN_ROWS
    return pl.pallas_call(
        gram_kernel,
        in_specs=[pl.BlockSpec(memory_space=pltpu.HBM)],
        out_specs=[pl.BlockSpec(memory_space=pltpu.VMEM)] * 4,
        out_shape=[jax.ShapeDtypeStruct((rows, BLOCK), jnp.float32)] * 4,
        scratch_shapes=[
            pltpu.VMEM((DEMES, GENS, LOCI), jnp.float32),
            pltpu.VMEM((CHUNK * GENS, 2 * LOCI), jnp.bfloat16),
            pltpu.VMEM((768, 256), jnp.float32),
            pltpu.VMEM((1024, 256), jnp.float32),
            pltpu.VMEM((GENS, LOCI), jnp.float32),
            pltpu.VMEM((GENS, LOCI), jnp.float32),
            pltpu.VMEM((PACKED, BLOCK), jnp.float32),
            pltpu.SemaphoreType.DMA((DEMES // CHUNK,)),
        ],
        compiler_params=pltpu.CompilerParams(vmem_limit_bytes=48 * MIB),
        name="local_gram",
    )(freqs)


def merge(refs, index, weight, packed, delta):
    rows = 4 * PIECE
    wide = [
        jnp.concatenate([ref[rows + 32 * j : rows + 32 * (j + 1), :] for j in range(4)], axis=1) for ref in refs
    ]
    mean = ((wide[0] + wide[2]) + (wide[1] + wide[3])) * 0.25
    for k, part in enumerate(wide):
        delta[pl.ds(pl.multiple_of(GENS * ((index + 4 - k) % 4), GENS), GENS), :] = part - mean
    for i in range(4):
        product = gram_of_few(delta[...], slice(BLOCK * i, BLOCK * (i + 1)))
        for j in range(i, 4):
            n = PAIRS.index((i, j))
            packed[BLOCK * n : BLOCK * (n + 1), :] = product[:, BLOCK * (j - i) : BLOCK * (j - i + 1)] * weight
    return mean


def merged_rows(refs, first, core, packed, out):
    for j in range(4):
        rows = slice(PIECE * j, PIECE * (j + 1))
        row = pl.multiple_of(piece_row(core, first, j), 8)
        out[rows, :] = ((refs[0][rows, :] + refs[2][rows, :]) + (refs[1][rows, :] + refs[3][rows, :])) + packed[
            pl.ds(row, PIECE), :
        ]


def first_kernel(*refs):
    ins, out, (packed, delta) = refs[:4], refs[4], refs[5:]
    first, second, core = place()
    mean = merge(ins, first, float(DEMES), packed, delta)
    merged_rows(ins, first, core, packed, out)
    for j in range(4):
        out[4 * PIECE + 32 * j : 4 * PIECE + 32 * (j + 1), :] = mean[:, BLOCK * j : BLOCK * (j + 1)]


def second_kernel(*refs):
    ins, (out, mean_out), (packed, delta) = refs[:4], refs[4:6], refs[6:]
    first, second, core = place()
    mean_out[...] = merge(ins, second, 4.0 * DEMES, packed, delta)
    merged_rows(ins, first, core, packed, out)


MERGE_SCRATCH = [pltpu.VMEM((PACKED, BLOCK), jnp.float32), pltpu.VMEM((4 * GENS, LOCI), jnp.float32)]


def merge_first(parts):
    return pl.pallas_call(
        first_kernel,
        out_shape=jax.ShapeDtypeStruct((4 * PIECE + MEAN_ROWS, BLOCK), jnp.float32),
        scratch_shapes=MERGE_SCRATCH,
        compiler_params=pltpu.CompilerParams(vmem_limit_bytes=16 * MIB),
        name="merge_first",
    )(*parts)


def merge_second(parts):
    return pl.pallas_call(
        second_kernel,
        out_shape=[
            jax.ShapeDtypeStruct((4 * PIECE, BLOCK), jnp.float32),
            jax.ShapeDtypeStruct((GENS, LOCI), jnp.float32),
        ],
        scratch_shapes=MERGE_SCRATCH,
        compiler_params=pltpu.CompilerParams(vmem_limit_bytes=16 * MIB),
        name="merge_second",
    )(*parts)


def inverse_cholesky(s):
    full = (8, RANK)
    lane = lax.broadcasted_iota(jnp.int32, full, 1)
    sub = lax.broadcasted_iota(jnp.int32, full, 0)
    count = RANK // 8
    rows = [s[8 * i : 8 * i + 8, :] for i in range(count)]

    def spread_row(value, j):
        return jnp.broadcast_to(value[j : j + 1, :], full)

    def spread_columns(i, k):
        return [jnp.broadcast_to(rows[i][:, 8 * k + j : 8 * k + j + 1], full) for j in range(8)]

    own_columns = spread_columns(0, 0)
    for k in range(count):
        here = (lane >= 8 * k) & (lane < 8 * k + 8)
        own = jnp.where(here, jnp.where(lane - 8 * k == sub, 1.0, 0.0), rows[k])
        last = k == count - 1
        if not last:
            near = spread_columns(k + 1, k)
            after = spread_columns(k + 1, k + 1)
            near_rows = jnp.where(here, 0.0, rows[k + 1])
        ratio, scaled, scale = {}, [], None
        for j in range(8):
            inverse = 1.0 / spread_row(own_columns[j], j)
            for l in range(j + 1, 8):
                ratio[l, j] = spread_row(own_columns[j], l) * inverse
                own_columns[l] = own_columns[l] - own_columns[j] * ratio[l, j]
            scaled.append(spread_row(own, j) * inverse)
            if j < 7:
                own = own - jnp.where(sub > j, own_columns[j], 0.0) * scaled[j]
            scale = jnp.where(sub == j, inverse, scale) if j else inverse
            if not last:
                near_rows = near_rows - near[j] * scaled[j]
                for l in range(8):
                    after[l] = after[l] - near[j] * (spread_row(near[j], l) * inverse)
                for l in range(j + 1, 8):
                    near[l] = near[l] - near[j] * ratio[l, j]
        solved = list(scaled)
        for j in range(7, 0, -1):
            for m in range(j):
                solved[m] = solved[m] - ratio[j, m] * solved[j]
        for i in range(k + 2, count):
            t = [column * part for column, part in zip(spread_columns(i, k), solved)]
            rows[i] = jnp.where(here, 0.0, rows[i]) - (
                ((t[0] + t[1]) + (t[2] + t[3])) + ((t[4] + t[5]) + (t[6] + t[7]))
            )
        rows[k] = jnp.where(lane <= 8 * k + sub, own * jnp.sqrt(scale), 0.0)
        if not last:
            rows[k + 1] = near_rows
            own_columns = after
    return jnp.concatenate(rows, axis=0)


def thirds(value):
    one = value.astype(jnp.bfloat16)
    value = value - one.astype(jnp.float32)
    two = value.astype(jnp.bfloat16)
    return one, two, (value - two.astype(jnp.float32)).astype(jnp.bfloat16)


def plain(a, b):
    return jnp.dot(a, b, preferred_element_type=jnp.float32)


def rows_product(a, b):
    return lax.dot_general(a, b, (((1,), (1,)), ((), ())), preferred_element_type=jnp.float32)


STEP = 32
STEPS = DEMES // STEP
LOADS = 4


def core_kernel(
    p0, p1, p2, p3, q0, q1, q2, q3, start_ref, mean_ref, x_hbm, core_hbm, factor_ref,
    x, core, packed, gram, gram_1, gram_2, gram_3, both, hi_a, lo_a, hi_b, lo_b, loads, stores,
):
    def load(n):
        part = pl.ds(n * (DEMES // LOADS), DEMES // LOADS)
        return pltpu.make_async_copy(x_hbm.at[part], x.at[part], loads.at[n])

    def store(n):
        part = pl.ds(n * STEP, STEP)
        return pltpu.make_async_copy(core.at[part], core_hbm.at[part], stores.at[n])

    for n in range(LOADS):
        load(n).start()

    first, second, core_id = place()
    for k, part in enumerate((p0, p1, p2, p3)):
        for l in range(4):
            row = pl.multiple_of(piece_row(core_id, (first + 4 - k) % 4, l), 8)
            packed[pl.ds(row, PIECE), :] = part[PIECE * l : PIECE * (l + 1), :]
    for k, part in enumerate((q0, q1, q2, q3)):
        for l in range(4):
            row = pl.multiple_of(piece_row(1 - core_id, (second + 4 - k) % 4, l), 8)
            packed[pl.ds(row, PIECE), :] += part[PIECE * l : PIECE * (l + 1), :]
    for n, (i, j) in enumerate(PAIRS):
        block = packed[BLOCK * n : BLOCK * (n + 1), :] * (1.0 / (4096 * 256))
        gram[BLOCK * i : BLOCK * (i + 1), BLOCK * j : BLOCK * (j + 1)] = block
        if i != j:
            gram[BLOCK * j : BLOCK * (j + 1), BLOCK * i : BLOCK * (i + 1)] = block.T

    gram_1[...], gram_2[...], gram_3[...] = thirds(gram[...])

    def body(_, basis):
        one, two, three = thirds(basis)
        by_first = plain(jnp.concatenate([one, two, three], axis=0), gram_1[...])
        by_second = plain(jnp.concatenate([one, two], axis=0), gram_2[...])
        z = by_first[:RANK] + (
            (by_first[RANK : 2 * RANK] + by_second[:RANK])
            + ((by_first[2 * RANK :] + by_second[RANK:]) + plain(one, gram_3[...]))
        )
        one, two, three = thirds(z)
        wide = rows_product(jnp.concatenate([one, two, three], axis=0), jnp.concatenate([one, two], axis=0))
        small = wide[:RANK, :RANK] + (
            (wide[RANK : 2 * RANK, :RANK] + wide[:RANK, RANK:])
            + ((wide[2 * RANK :, :RANK] + rows_product(one, three)) + wide[RANK : 2 * RANK, RANK:])
        )
        w_one, w_two, w_three = thirds(inverse_cholesky(small))
        w_pair = jnp.concatenate([w_one, w_two], axis=1)
        large = plain(w_pair, jnp.concatenate([one, one], axis=0))
        middle = plain(w_pair, jnp.concatenate([two, two], axis=0))
        rest = plain(jnp.concatenate([w_one, w_three], axis=1), jnp.concatenate([three, one], axis=0))
        return large + (middle + rest)

    basis = lax.fori_loop(0, ITERS, body, start_ref[...].T)
    factor = basis.T
    factor_ref[...] = factor
    hi = factor.astype(jnp.bfloat16)
    both[:, :RANK] = hi
    both[:, RANK:] = (factor - hi.astype(jnp.float32)).astype(jnp.bfloat16)
    for n in range(LOADS):
        load(n).wait()

    def split(n, d_hi, d_lo):
        d = (x[pl.ds(n * STEP, STEP)] - mean_ref[...][None]).reshape(STEP * GENS, LOCI)
        d_hi[...] = d.astype(jnp.bfloat16)
        d_lo[...] = (d - d.astype(jnp.bfloat16).astype(jnp.float32)).astype(jnp.bfloat16)

    def multiply(n, d_hi, d_lo):
        wide = jnp.dot(d_hi[...], both[...], preferred_element_type=jnp.float32)
        rest = jnp.dot(d_lo[...], both[:, :RANK], preferred_element_type=jnp.float32)
        core[pl.ds(n * STEP, STEP)] = (wide[:, :RANK] + (wide[:, RANK:] + rest)).reshape(STEP, GENS, RANK)

    def pair(p, carry):
        split(2 * p + 1, hi_b, lo_b)
        multiply(2 * p, hi_a, lo_a)
        store(2 * p).start()
        split(jnp.minimum(2 * p + 2, STEPS - 1), hi_a, lo_a)
        multiply(2 * p + 1, hi_b, lo_b)
        store(2 * p + 1).start()
        return carry

    split(0, hi_a, lo_a)
    lax.fori_loop(0, STEPS // 2, pair, 0)
    for n in range(STEPS):
        store(n).wait()


def iterate(parts, start_basis, mean, freqs):
    vmem = pl.BlockSpec(memory_space=pltpu.VMEM)
    hbm = pl.BlockSpec(memory_space=pltpu.HBM)
    return pl.pallas_call(
        core_kernel,
        in_specs=[vmem] * 10 + [hbm],
        out_specs=[hbm, vmem],
        out_shape=[
            jax.ShapeDtypeStruct((DEMES, GENS, RANK), jnp.float32),
            jax.ShapeDtypeStruct((LOCI, RANK), jnp.float32),
        ],
        scratch_shapes=[
            pltpu.VMEM((DEMES, GENS, LOCI), jnp.float32),
            pltpu.VMEM((DEMES, GENS, RANK), jnp.float32),
            pltpu.VMEM((PACKED, BLOCK), jnp.float32),
            pltpu.VMEM((LOCI, LOCI), jnp.float32),
            pltpu.VMEM((LOCI, LOCI), jnp.bfloat16),
            pltpu.VMEM((LOCI, LOCI), jnp.bfloat16),
            pltpu.VMEM((LOCI, LOCI), jnp.bfloat16),
            pltpu.VMEM((LOCI, 2 * RANK), jnp.bfloat16),
        ]
        + [pltpu.VMEM((STEP * GENS, LOCI), jnp.bfloat16)] * 4
        + [
            pltpu.SemaphoreType.DMA((LOADS,)),
            pltpu.SemaphoreType.DMA((STEPS,)),
        ],
        compiler_params=pltpu.CompilerParams(vmem_limit_bytes=48 * MIB),
        name="iterate",
    )(*parts, start_basis, mean, freqs)


def local(freqs, start_basis):
    out = local_gram(freqs)
    rows = merge_first([out[0]] + [send(out[k], "first", k) for k in (1, 2, 3)])
    rows, mean = merge_second([rows] + [send(rows, "second", k) for k in (1, 2, 3)])
    one, two, three = [send(rows, "x", k) for k in (1, 2, 3)]
    rows = (rows + two) + (one + three)
    parts = [rows] + [send(rows, "first", k) for k in (1, 2, 3)]
    parts += [send(part, "core", 1) for part in parts]
    return tuple(iterate(parts, start_basis, mean, freqs))


def solution(mesh):
    in_specs = (P("deme", "gen", None), P())
    out_specs = (P("deme", "gen", None), P())
    return jax.shard_map(local, mesh=mesh, in_specs=in_specs, out_specs=out_specs, check_vma=False)
```
